32 devices in a mesh: wide: 8 (over z, x), narrow: 4 (over y, core).
Axes of the slice: x: 2, y: 2, z: 4, core: 2. Of those that a mesh axis runs over, the one named last changes fastest.
Arguments:
- front: bfloat16 [16, 8, 128, 32, 4, 128], P(None, 'wide', None, None, 'narrow'), may hold values from -6 to 6
- pivot_inverse: bfloat16 [4, 128, 128], replicated, may hold values from -0.0105112052 to 0.17838107
- rhs: bfloat16 [16, 8, 128, 256], P(None, 'wide'), may hold values from -6 to 6
- trail_sol: bfloat16 [16, 8, 128, 256], P(None, 'wide'), may hold values from -1.1953125 to 1.1953125
- block_mask: int32 [16, 8, 32, 4], P(None, 'wide', None, 'narrow'), may hold values 0 or 1
- panel_order: int32 [4], replicated, may hold values from 0 to 3, each once
Outputs:
- front_out: bfloat16 [16, 8, 128, 32, 4, 128], P(None, 'wide', None, None, 'narrow')
- forward_rhs: bfloat16 [16, 8, 128, 256], P(None, 'wide')
- window_solution: bfloat16 [4, 128, 256], replicated
The draws below stay inside these ranges and needn't reach their ends.
Inputs may be any that keep to these rules, and one draw needn't show every extreme that they name: `panel_order`: each value 0 to 3 appears once.
All inputs are finite; a program needn't handle non-finite values. No bound on the sum of `block_mask` on one device may be relied on, other than what follows from the above.
Results may differ from the reference program's by a relative error of at most 0.0076.
Values may be sent and summed in bfloat16 or wider, within the bound.
A program may use at most 128 MiB of HBM per device.

```python
import math
import jax
import jax.numpy as jnp
from jax import lax

BS = 128
NBLK = 128
NRHS = 256
PANELS = 4
RLOC = 16
CLOC = 32
N_WIDE = 8
N_NARROW = 4


def draw_pivot_inverse(key, part):
    inner = jax.random.fold_in(key, 7177)
    key_diag, key_off = jax.random.split(inner)
    scale = 0.5 * BS ** (-0.25)
    spread = 0.2 / math.sqrt(BS)
    diag = jax.random.uniform(key_diag, (PANELS, BS), jnp.float32, 0.9, 1.1)
    noise = jnp.clip(jax.random.normal(key_off, (PANELS, BS, BS), jnp.float32), -4.0, 4.0) * spread
    rows_index = lax_iota_rows()
    cols_index = lax_iota_cols()
    on_diag = (rows_index == cols_index)[None, :, :]
    matrix = jnp.where(on_diag, diag[:, :, None], noise)
    return (scale * matrix).astype(jnp.bfloat16)


def lax_iota_rows():
    return jnp.arange(BS, dtype=jnp.int32)[:, None] + jnp.zeros((1, BS), jnp.int32)


def lax_iota_cols():
    return jnp.arange(BS, dtype=jnp.int32)[None, :] + jnp.zeros((BS, 1), jnp.int32)


def set_ends(array, rng, least, high):
    index_at = [jax.random.randint(jax.random.fold_in(rng, axis), (), 0, length) for axis, length in enumerate(array.shape)]
    main_axis = array.shape.index(max(array.shape))
    neighbour = index_at[:main_axis] + [(index_at[main_axis] + 1) % array.shape[main_axis]] + index_at[main_axis + 1:]
    return array.at[tuple(index_at)].set(least).at[tuple(neighbour)].set(high)


def level_of(key, dims, cuts, least, largest):
    loudness, own = 1.0, jax.random.fold_in(key, 6)
    for axis_at, blocks in cuts:
        heights = jnp.exp(jax.random.uniform(jax.random.fold_in(own, axis_at), (blocks,), jnp.float32, least / len(cuts), largest / len(cuts)))
        loudness = loudness * jnp.repeat(heights, dims[axis_at] // blocks).reshape([-1 if axis == axis_at else 1 for axis in range(len(dims))])
    return loudness


def centred(stream_key, shape, scale, limit, pieces=(), kind=jnp.bfloat16):
    loudness = level_of(stream_key, shape, pieces, -0.22, 0.18) if pieces else 1.0
    array = jax.random.normal(stream_key, shape, jnp.float32) * scale * loudness
    return jnp.minimum(jnp.maximum(array, -limit), limit).astype(kind)


def setup_inputs(seed: int = 0) -> dict:
    key_of = jax.random.split(jax.random.key(seed), 7)
    front = centred(key_of[0], (RLOC, N_WIDE, BS, CLOC, N_NARROW, BS), 1.0, 6.0, ((1, 8), (4, 4)))
    pivot_inverse = draw_pivot_inverse(jax.random.fold_in(key_of[6], 71), 0)
    rhs = centred(key_of[2], (RLOC, N_WIDE, BS, NRHS), 1.0, 6.0, ((1, 8),))
    trail_sol = centred(key_of[3], (RLOC, N_WIDE, BS, NRHS), 0.2, 1.1953125, ((1, 8),))
    block_mask = set_ends((jax.random.randint(key_of[4], (RLOC, N_WIDE, CLOC, N_NARROW), 0, 5) < 4).astype(jnp.int32), jax.random.fold_in(key_of[4], 1), 0, 1)
    panel_order = jax.random.permutation(key_of[5], PANELS).astype(jnp.int32)
    return {"front": front, "pivot_inverse": pivot_inverse, "rhs": rhs, "trail_sol": trail_sol, "block_mask": block_mask, "panel_order": panel_order}


def reference(front, pivot_inverse, rhs, trail_sol, block_mask, panel_order):
    blocks = front.reshape(NBLK, BS, NBLK, BS)
    pattern = block_mask.reshape(NBLK, NBLK).astype(jnp.float32)
    right = rhs.reshape(NBLK, BS, NRHS)
    trailing = trail_sol.reshape(NBLK, BS, NRHS)
    ranks = jnp.full((NBLK,), PANELS, jnp.int32).at[panel_order].set(jnp.arange(PANELS, dtype=jnp.int32))
    saved_left = []
    saved_pivot = []
    for section in range(PANELS):
        target = panel_order[section]
        weight = lax.dynamic_index_in_dim(pivot_inverse, target, 0, keepdims=False).astype(jnp.float32)
        alive = ranks > section
        column = lax.dynamic_index_in_dim(blocks, target, 2, keepdims=False).astype(jnp.float32)
        left = jnp.einsum('iab,bc->iac', column, weight)
        left = jnp.where(alive[:, None, None], left, 0.0).astype(jnp.bfloat16)
        row_blocks = lax.dynamic_index_in_dim(blocks, target, 0, keepdims=False).astype(jnp.float32)
        upper = jnp.einsum('ac,ajb->cjb', weight, row_blocks)
        upper = jnp.where(alive[None, :, None], upper, 0.0).astype(jnp.bfloat16)
        upper_f = upper.astype(jnp.float32)

        def update_one(packed):
            a_row, l_row, m_row = packed
            product = jnp.einsum('ac,cjb->ajb', l_row.astype(jnp.float32), upper_f)
            return (a_row.astype(jnp.float32) - m_row[None, :, None] * product).astype(jnp.bfloat16)

        blocks = lax.map(update_one, (blocks, left, pattern))
        pivot_rhs = lax.dynamic_index_in_dim(right, target, 0, keepdims=False).astype(jnp.float32)
        solved = jnp.einsum('ac,an->cn', weight, pivot_rhs).astype(jnp.bfloat16)
        right = (right.astype(jnp.float32) - jnp.einsum('iac,cn->ian', left.astype(jnp.float32), solved.astype(jnp.float32))).astype(jnp.bfloat16)
        saved_left.append(left)
        saved_pivot.append(solved)
    current = trailing
    window = jnp.zeros((PANELS, BS, NRHS), jnp.bfloat16)
    for section in reversed(range(PANELS)):
        target = panel_order[section]
        weight = lax.dynamic_index_in_dim(pivot_inverse, target, 0, keepdims=False).astype(jnp.float32)
        total = jnp.einsum('iac,ian->cn', saved_left[section].astype(jnp.float32), current.astype(jnp.float32))
        corrected = (saved_pivot[section].astype(jnp.float32) - total).astype(jnp.bfloat16)
        result = jnp.einsum('ac,cn->an', weight, corrected.astype(jnp.float32)).astype(jnp.bfloat16)
        current = lax.dynamic_update_index_in_dim(current, result, target, 0)
        window = lax.dynamic_update_index_in_dim(window, result, target, 0)
    return blocks.reshape(front.shape), right.reshape(rhs.shape), window
```

```python
import functools

import jax
import jax.numpy as jnp
from jax import lax
from jax.experimental import pallas as pl
from jax.experimental.pallas import tpu as pltpu
from jax.sharding import PartitionSpec as P

PIECES = 8


def greet(nwide, nnarrow):
    w, q = lax.axis_index("wide"), lax.axis_index("narrow")
    barrier = pltpu.get_barrier_semaphore()
    for step in range(1, nwide):
        pl.semaphore_signal(
            barrier, inc=1, device_id={"wide": lax.rem(w + step, nwide)},
            device_id_type=pl.DeviceIdType.MESH,
        )
    for step in range(1, nnarrow):
        pl.semaphore_signal(
            barrier, inc=1, device_id={"narrow": lax.rem(q + step, nnarrow)},
            device_id_type=pl.DeviceIdType.MESH,
        )
    pl.semaphore_wait(barrier, nwide + nnarrow - 2)


def remote(src, dst, send, recv, axis, index):
    return pltpu.make_async_remote_copy(
        src_ref=src, dst_ref=dst, send_sem=send, recv_sem=recv,
        device_id={axis: index}, device_id_type=pl.DeviceIdType.MESH,
    )


def gather_kernel(
    nwide, nnarrow,
    front, rhs, col, colmask, rowmask,
    rows, heads, rmask, pivots, cols, cmask, wins, wmask,
    own_sem, up_send, down_send, cross_send, line_recv, cross_recv,
    side_send, side_recv, side_own,
):
    w, q = lax.axis_index("wide"), lax.axis_index("narrow")
    lines = nwide // 2
    a, b = w // 2, lax.rem(w, 2)
    cut = front.shape[1] // PIECES

    items = [
        (col.at[0], lambda k: heads.at[k]),
        (rowmask, lambda k: rmask.at[k]),
    ]
    for piece in range(PIECES):
        at = pl.ds(piece * cut, cut)
        items.append((front.at[0, at], lambda k, at=at: rows.at[k, at]))
    items.append((rhs.at[0], lambda k: pivots.at[k]))

    def own(i):
        return pltpu.make_async_copy(items[i][0], items[i][1](w), own_sem.at[i])

    def line(i, s, to, send):
        slot = items[i][1](2 * s + b)
        return remote(slot, slot, send.at[i, s], line_recv.at[i, s], "wide", to)

    def up(i, s):
        return line(i, s, 2 * lax.rem(a + 1, lines) + b, up_send)

    def down(i):
        return line(i, 1, b, down_send)

    def cross(i, s, column):
        slot = items[i][1](2 * s + column)
        return remote(
            slot, slot, cross_send.at[i, s], cross_recv.at[i, s], "wide", 2 * a + 1 - b
        )

    def side(i, step):
        src, slots = side_items[i]
        slot = slots(q)
        peer = lax.rem(q + step, nnarrow)
        return remote(src, slot, side_send.at[i, step], side_recv.at[i, step], "narrow", peer)

    def side_in(i, step):
        src, slots = side_items[i]
        sender = lax.rem(q + nnarrow - step, nnarrow)
        return remote(src, slots(sender), side_send.at[i, step], side_recv.at[i, step], "narrow", sender)

    def side_self(i):
        src, slots = side_items[i]
        return pltpu.make_async_copy(src, slots(q), side_own.at[i])

    side_items = [
        (col, lambda n: cols.at[n]),
        (colmask, lambda n: cmask.at[n]),
        (heads, lambda n: wins.at[n]),
        (rmask.at[:, pl.ds(0, 8)], lambda n: wmask.at[n]),
    ]

    greet(nwide, nnarrow)

    @pl.when(a < 2)
    def _():
        for i in range(len(items)):
            own(i).start()

    def relay(i):
        for s in (0, 1):
            @pl.when(a == s)
            def _():
                own(i).wait()

            @pl.when(a != s)
            def _():
                up(i, s).wait_recv()

            if lines > 1:
                @pl.when((a + 1 < lines) & (a >= s))
                def _():
                    up(i, s).start()

                if s == 1:
                    @pl.when(a == 1)
                    def _():
                        down(i).start()

            cross(i, s, b).start()

    def side_start(i):
        side_self(i).start()
        for step in range(1, nnarrow):
            side(i, step).start()

    def crossed(i):
        for s in (0, 1):
            cross(i, s, 1 - b).wait_recv()

    relay(0)
    relay(1)
    side_start(0)
    side_start(1)
    relay(2)
    for i in (0, 1):
        crossed(i)
    side_start(2)
    side_start(3)
    for i in range(3, len(items)):
        relay(i)
    for i in range(2, len(items)):
        crossed(i)
    for i in range(len(side_items)):
        side_self(i).wait()
        for step in range(1, nnarrow):
            side_in(i, step).wait_recv()
            side(i, step).wait_send()
    for i in range(len(items)):
        for s in (0, 1):
            cross(i, s, b).wait_send()

            @pl.when((a + 1 < lines) & (a >= s))
            def _():
                up(i, s).wait_send()

        @pl.when(a == 1)
        def _():
            down(i).wait_send()


def gather(front, rhs, col, colmask, rowmask, panels):
    nwide, nnarrow = lax.axis_size("wide"), lax.axis_size("narrow")
    rloc, bsize, cloc, _ = front.shape
    nrhs = rhs.shape[2]
    bf, f32 = jnp.bfloat16, jnp.float32
    n = PIECES + 3
    dma = pltpu.SemaphoreType.DMA
    any_spec = pl.BlockSpec(memory_space=pl.ANY)
    return pl.pallas_call(
        functools.partial(gather_kernel, nwide, nnarrow),
        out_shape=(
            jax.ShapeDtypeStruct((panels, bsize, cloc, bsize), bf),
            jax.ShapeDtypeStruct((panels, bsize, bsize), bf),
            jax.ShapeDtypeStruct((panels, cloc, 128), f32),
            jax.ShapeDtypeStruct((panels, bsize, nrhs), bf),
            jax.ShapeDtypeStruct((nnarrow, rloc, bsize, bsize), bf),
            jax.ShapeDtypeStruct((nnarrow, rloc, 128), f32),
            jax.ShapeDtypeStruct((nnarrow, panels, bsize, bsize), bf),
            jax.ShapeDtypeStruct((nnarrow, panels, 8, 128), f32),
        ),
        in_specs=[any_spec] * 5,
        out_specs=(any_spec,) * 8,
        scratch_shapes=[
            dma((n,)), dma((n, 2)), dma((n, 2)), dma((n, 2)), dma((n, 2)), dma((n, 2)),
            dma((4, nnarrow)), dma((4, nnarrow)), dma((4,)),
        ],
        compiler_params=pltpu.CompilerParams(collective_id=0, has_side_effects=True),
        name="gather_panels",
    )(front, rhs, col, colmask, rowmask)


def reduce_kernel(
    nwide, nnarrow, part, total, landing, send1, recv1, send2, recv2, send3, recv3,
):
    w, q = lax.axis_index("wide"), lax.axis_index("narrow")
    greet(nwide, nnarrow)

    def give(step):
        peer = lax.rem(w + step, nwide)
        return remote(part.at[q, peer], landing.at[step], send1.at[step], recv1.at[step], "wide", peer)

    def spread(step):
        peer = lax.rem(w + step, nwide)
        return remote(total.at[q, w], total.at[q, w], send2.at[step], recv2.at[step], "wide", peer)

    def spread_in(step):
        sender = lax.rem(w + nwide - step, nwide)
        return remote(total.at[q, sender], total.at[q, sender], send2.at[step], recv2.at[step], "wide", sender)

    def pass_on(step):
        peer = lax.rem(q + step, nnarrow)
        return remote(total.at[q], total.at[q], send3.at[step], recv3.at[step], "narrow", peer)

    def pass_in(step):
        sender = lax.rem(q + nnarrow - step, nnarrow)
        return remote(total.at[sender], total.at[sender], send3.at[step], recv3.at[step], "narrow", sender)

    for step in range(1, nwide):
        give(step).start()
    acc = part[q, w]
    for step in range(1, nwide):
        give(step).wait_recv()
        acc = acc + landing[step]
    total[q, w] = acc
    for step in range(1, nwide):
        spread(step).start()
    for step in range(1, nwide):
        spread_in(step).wait_recv()
    for step in range(1, nnarrow):
        pass_on(step).start()
    for step in range(1, nnarrow):
        pass_in(step).wait_recv()
    for step in range(1, nwide):
        give(step).wait_send()
        spread(step).wait_send()
    for step in range(1, nnarrow):
        pass_on(step).wait_send()


def reduce_sums(part):
    nwide, nnarrow = lax.axis_size("wide"), lax.axis_size("narrow")
    shape = part.shape
    rows = shape[0] * shape[1] // (nwide * nnarrow)
    split = (nnarrow, nwide, rows, shape[2])
    dma = pltpu.SemaphoreType.DMA
    vmem = pl.BlockSpec(memory_space=pltpu.VMEM)
    total = pl.pallas_call(
        functools.partial(reduce_kernel, nwide, nnarrow),
        out_shape=jax.ShapeDtypeStruct(split, jnp.float32),
        in_specs=[vmem],
        out_specs=vmem,
        scratch_shapes=[
            pltpu.VMEM((nwide, rows, shape[2]), jnp.float32),
            dma((nwide,)), dma((nwide,)), dma((nwide,)), dma((nwide,)),
            dma((nnarrow,)), dma((nnarrow,)),
        ],
        compiler_params=pltpu.CompilerParams(collective_id=1, has_side_effects=True),
        name="reduce_sums",
    )(part.reshape(split))
    return total.reshape(shape)


def body(front, pivot_inverse, rhs, trail_sol, block_mask, panel_order):
    rloc, bsize, cloc = front.shape[0], front.shape[2], front.shape[3]
    nrhs = rhs.shape[3]
    panels = panel_order.shape[0]
    nwide, nnarrow = lax.axis_size("wide"), lax.axis_size("narrow")
    f32, bf = jnp.float32, jnp.bfloat16
    blocks = front.reshape(rloc, bsize, cloc, bsize)
    pattern = block_mask.reshape(rloc, cloc).astype(f32)
    right = rhs.reshape(rloc, bsize, nrhs)
    trail = trail_sol.reshape(rloc, bsize, nrhs)
    ids = jnp.arange(panels, dtype=jnp.int32)
    rank = jnp.sum(jnp.where(panel_order[None, :] == ids[:, None], ids[None, :], 0), axis=1)
    rows_global = jnp.arange(rloc, dtype=jnp.int32) * nwide + lax.axis_index("wide")
    cols_global = jnp.arange(cloc, dtype=jnp.int32) * nnarrow + lax.axis_index("narrow")

    def rank_of(index):
        return jnp.min(
            jnp.where(index[:, None] == panel_order[None, :], ids[None, :], panels), axis=1
        )

    rows_rank, cols_rank = rank_of(rows_global), rank_of(cols_global)

    col = blocks[:, :, 0, :]
    colmask = jnp.broadcast_to(pattern[:, :1], (rloc, 128))
    rowmask = jnp.broadcast_to(pattern[0][:, None], (cloc, 128))
    rows, _, rmask, pivots, cols, cmask, wins, wmask = gather(
        blocks, right, col, colmask, rowmask, panels
    )
    dot = functools.partial(jnp.einsum, preferred_element_type=f32)
    cmask = cmask[:, :, 0]
    rmask = rmask[:, :, 0]
    wmask = wmask[:, :, 0, 0]

    def pick(array, index):
        return lax.dynamic_index_in_dim(array, index, 0, keepdims=False)

    def minus(old, change):
        return (old.astype(f32) - change).astype(bf)

    lefts, win_lefts, uppers, solves = [], [], [], []
    for s in range(panels):
        k = panel_order[s]
        weight = pick(pivot_inverse, k)
        alive = rank > s
        left = dot("rab,bc->rac", pick(cols, k), weight)
        left = jnp.where((rows_rank > s)[:, None, None], left, 0.0).astype(bf)
        win_left = dot("rab,bc->rac", pick(wins, k), weight)
        win_left = jnp.where(alive[:, None, None], win_left, 0.0).astype(bf)
        win_upper = dot("ac,qab->qcb", weight, lax.dynamic_index_in_dim(wins, k, 1, keepdims=False))
        win_upper = jnp.where(alive[:, None, None], win_upper, 0.0).astype(bf)
        upper = dot("ac,ajb->cjb", weight, pick(rows, k))
        upper = jnp.where((cols_rank > s)[None, :, None], upper, 0.0).astype(bf)
        solved = dot("ac,an->cn", weight, pick(pivots, k)).astype(bf)
        if s + 1 < panels:
            cols = minus(cols, cmask[:, :, None, None] * dot("rac,qcb->qrab", left, win_upper))
            wins = minus(wins, wmask[:, :, None, None] * dot("rac,qcb->qrab", win_left, win_upper))
            rows = minus(rows, rmask[:, None, :, None] * dot("rac,cjb->rajb", win_left, upper))
            pivots = minus(pivots, dot("rac,cn->ran", win_left, solved))
        lefts.append(left)
        win_lefts.append(win_left)
        uppers.append(upper)
        solves.append(solved)
    left = jnp.concatenate(lefts, axis=2)
    trail = jnp.where((rows_global >= panels)[:, None, None], trail, jnp.zeros_like(trail))
    sums = dot("rak,ran->kn", left, trail).reshape(panels, bsize, nrhs)
    sums = reduce_sums(sums)
    product = dot("rak,kjb->rajb", left, jnp.concatenate(uppers, axis=0))
    blocks = minus(blocks, pattern[:, None, :, None] * product)
    right = minus(right, dot("rak,kn->ran", left, jnp.concatenate(solves, axis=0)))
    window = jnp.zeros((panels, bsize, nrhs), bf)
    for s in reversed(range(panels)):
        total = sums[s] + dot("iac,ian->cn", win_lefts[s], window)
        corrected = (solves[s].astype(f32) - total).astype(bf)
        result = dot("ac,cn->an", pick(pivot_inverse, panel_order[s]), corrected).astype(bf)
        window = lax.dynamic_update_index_in_dim(window, result, panel_order[s], 0)
    return (blocks.reshape(front.shape), right.reshape(rhs.shape), window)


def solution(mesh):
    in_specs = (
        P(None, "wide", None, None, "narrow", None),
        P(),
        P(None, "wide", None, None),
        P(None, "wide", None, None),
        P(None, "wide", None, "narrow"),
        P(),
    )
    out_specs = (P(None, "wide", None, None, "narrow", None), P(None, "wide", None, None), P())
    return jax.shard_map(body, mesh=mesh, in_specs=in_specs, out_specs=out_specs, check_vma=False)
```

```python
import functools

import jax
import jax.numpy as jnp
from jax import lax
from jax.experimental import pallas as pl
from jax.experimental.pallas import tpu as pltpu
from jax.sharding import PartitionSpec as P

PIECES = 8
CHUNK = 1024
GROUP = 4


def greet(nwide, nnarrow):
    w, q = lax.axis_index("wide"), lax.axis_index("narrow")
    barrier = pltpu.get_barrier_semaphore()
    for step in range(1, nwide):
        pl.semaphore_signal(
            barrier, inc=1, device_id={"wide": lax.rem(w + step, nwide)},
            device_id_type=pl.DeviceIdType.MESH,
        )
    for step in range(1, nnarrow):
        pl.semaphore_signal(
            barrier, inc=1, device_id={"narrow": lax.rem(q + step, nnarrow)},
            device_id_type=pl.DeviceIdType.MESH,
        )
    pl.semaphore_wait(barrier, nwide + nnarrow - 2)


def remote(src, dst, send, recv, axis, index):
    return pltpu.make_async_remote_copy(
        src_ref=src, dst_ref=dst, send_sem=send, recv_sem=recv,
        device_id={axis: index}, device_id_type=pl.DeviceIdType.MESH,
    )


def gather_kernel(
    nwide, nnarrow,
    front, rhs, col, colmask, rowmask,
    rows, heads, rmask, pivots, cols, cmask, wins, wmask,
    own_sem, up_send, down_send, cross_send, line_recv, cross_recv,
    side_send, side_recv, side_own,
):
    w, q = lax.axis_index("wide"), lax.axis_index("narrow")
    lines = nwide // 2
    a, b = w // 2, lax.rem(w, 2)
    cut = front.shape[1] // PIECES

    items = [
        (col.at[0], lambda k: heads.at[k]),
        (rowmask, lambda k: rmask.at[k]),
    ]
    for piece in range(PIECES):
        at = pl.ds(piece * cut, cut)
        items.append((front.at[:, at], lambda k, at=at: rows.at[k, :, at]))
    items.append((rhs.at[0], lambda k: pivots.at[k]))

    def own(i):
        return pltpu.make_async_copy(items[i][0], items[i][1](w), own_sem.at[i])

    def line(i, s, to, send):
        slot = items[i][1](2 * s + b)
        return remote(slot, slot, send.at[i, s], line_recv.at[i, s], "wide", to)

    def up(i, s):
        return line(i, s, 2 * lax.rem(a + 1, lines) + b, up_send)

    def down(i):
        return line(i, 1, b, down_send)

    def cross(i, s, column):
        slot = items[i][1](2 * s + column)
        return remote(
            slot, slot, cross_send.at[i, s], cross_recv.at[i, s], "wide", 2 * a + 1 - b
        )

    def side(i, step):
        src, slots = side_items[i]
        slot = slots(q)
        peer = lax.rem(q + step, nnarrow)
        return remote(src, slot, side_send.at[i, step], side_recv.at[i, step], "narrow", peer)

    def side_in(i, step):
        src, slots = side_items[i]
        sender = lax.rem(q + nnarrow - step, nnarrow)
        return remote(src, slots(sender), side_send.at[i, step], side_recv.at[i, step], "narrow", sender)

    def side_self(i):
        src, slots = side_items[i]
        return pltpu.make_async_copy(src, slots(q), side_own.at[i])

    side_items = [
        (col, lambda n: cols.at[n]),
        (colmask, lambda n: cmask.at[n]),
        (heads, lambda n: wins.at[n]),
        (rmask.at[:, pl.ds(0, 8)], lambda n: wmask.at[n]),
    ]

    greet(nwide, nnarrow)

    @pl.when(a < 2)
    def _():
        for i in range(len(items)):
            own(i).start()

    def relay(i):
        for s in (0, 1):
            @pl.when(a == s)
            def _():
                own(i).wait()

            @pl.when(a != s)
            def _():
                up(i, s).wait_recv()

            if lines > 1:
                @pl.when((a + 1 < lines) & (a >= s))
                def _():
                    up(i, s).start()

                if s == 1:
                    @pl.when(a == 1)
                    def _():
                        down(i).start()

            cross(i, s, b).start()

    def side_start(i):
        side_self(i).start()
        for step in range(1, nnarrow):
            side(i, step).start()

    def crossed(i):
        for s in (0, 1):
            cross(i, s, 1 - b).wait_recv()

    relay(0)
    relay(1)
    side_start(0)
    side_start(1)
    relay(2)
    for i in (0, 1):
        crossed(i)
    side_start(2)
    side_start(3)
    for i in range(3, len(items)):
        relay(i)
    for i in range(2, len(items)):
        crossed(i)
    for i in range(len(side_items)):
        side_self(i).wait()
        for step in range(1, nnarrow):
            side_in(i, step).wait_recv()
            side(i, step).wait_send()
    for i in range(len(items)):
        for s in (0, 1):
            cross(i, s, b).wait_send()

            @pl.when((a + 1 < lines) & (a >= s))
            def _():
                up(i, s).wait_send()

        @pl.when(a == 1)
        def _():
            down(i).wait_send()


def gather(front, rhs, col, colmask, rowmask, panels):
    nwide, nnarrow = lax.axis_size("wide"), lax.axis_size("narrow")
    rloc, bsize, nrhs = rhs.shape
    cloc = front.shape[1] // bsize
    bf, f32 = jnp.bfloat16, jnp.float32
    n = PIECES + 3
    dma = pltpu.SemaphoreType.DMA
    any_spec = pl.BlockSpec(memory_space=pl.ANY)
    return pl.pallas_call(
        functools.partial(gather_kernel, nwide, nnarrow),
        out_shape=(
            jax.ShapeDtypeStruct((panels, bsize, cloc * bsize), bf),
            jax.ShapeDtypeStruct((panels, bsize, bsize), bf),
            jax.ShapeDtypeStruct((panels, cloc, 128), f32),
            jax.ShapeDtypeStruct((panels, bsize, nrhs), bf),
            jax.ShapeDtypeStruct((nnarrow, rloc, bsize, bsize), bf),
            jax.ShapeDtypeStruct((nnarrow, rloc, 128), f32),
            jax.ShapeDtypeStruct((nnarrow, panels, bsize, bsize), bf),
            jax.ShapeDtypeStruct((nnarrow, panels, 8, 128), f32),
        ),
        in_specs=[any_spec] * 5,
        out_specs=(any_spec,) * 8,
        scratch_shapes=[
            dma((n,)), dma((n, 2)), dma((n, 2)), dma((n, 2)), dma((n, 2)), dma((n, 2)),
            dma((4, nnarrow)), dma((4, nnarrow)), dma((4,)),
        ],
        compiler_params=pltpu.CompilerParams(collective_id=0, has_side_effects=True),
        name="gather_panels",
    )(front, rhs, col, colmask, rowmask)


def reduce_kernel(
    nwide, nnarrow, part, total, landing, send1, recv1, send2, recv2, send3, recv3,
):
    w, q = lax.axis_index("wide"), lax.axis_index("narrow")
    greet(nwide, nnarrow)

    def give(step):
        peer = lax.rem(w + step, nwide)
        return remote(part.at[q, peer], landing.at[step], send1.at[step], recv1.at[step], "wide", peer)

    def spread(step):
        peer = lax.rem(w + step, nwide)
        return remote(total.at[q, w], total.at[q, w], send2.at[step], recv2.at[step], "wide", peer)

    def spread_in(step):
        sender = lax.rem(w + nwide - step, nwide)
        return remote(total.at[q, sender], total.at[q, sender], send2.at[step], recv2.at[step], "wide", sender)

    def pass_on(step):
        peer = lax.rem(q + step, nnarrow)
        return remote(total.at[q], total.at[q], send3.at[step], recv3.at[step], "narrow", peer)

    def pass_in(step):
        sender = lax.rem(q + nnarrow - step, nnarrow)
        return remote(total.at[sender], total.at[sender], send3.at[step], recv3.at[step], "narrow", sender)

    for step in range(1, nwide):
        give(step).start()
    acc = part[q, w]
    for step in range(1, nwide):
        give(step).wait_recv()
        acc = acc + landing[step]
    total[q, w] = acc
    for step in range(1, nwide):
        spread(step).start()
    for step in range(1, nwide):
        spread_in(step).wait_recv()
    for step in range(1, nnarrow):
        pass_on(step).start()
    for step in range(1, nnarrow):
        pass_in(step).wait_recv()
    for step in range(1, nwide):
        give(step).wait_send()
        spread(step).wait_send()
    for step in range(1, nnarrow):
        pass_on(step).wait_send()


def reduce_sums(part):
    nwide, nnarrow = lax.axis_size("wide"), lax.axis_size("narrow")
    shape = part.shape
    rows = shape[0] * shape[1] // (nwide * nnarrow)
    split = (nnarrow, nwide, rows, shape[2])
    dma = pltpu.SemaphoreType.DMA
    vmem = pl.BlockSpec(memory_space=pltpu.VMEM)
    total = pl.pallas_call(
        functools.partial(reduce_kernel, nwide, nnarrow),
        out_shape=jax.ShapeDtypeStruct(split, jnp.float32),
        in_specs=[vmem],
        out_specs=vmem,
        scratch_shapes=[
            pltpu.VMEM((nwide, rows, shape[2]), jnp.float32),
            dma((nwide,)), dma((nwide,)), dma((nwide,)), dma((nwide,)),
            dma((nnarrow,)), dma((nnarrow,)),
        ],
        compiler_params=pltpu.CompilerParams(collective_id=1, has_side_effects=True),
        name="reduce_sums",
    )(part.reshape(split))
    return total.reshape(shape)


def mm(x, y):
    return jnp.dot(x, y, preferred_element_type=jnp.float32)


def mm_t(x, y):
    return lax.dot_general(x, y, (((0,), (0,)), ((), ())), preferred_element_type=jnp.float32)


def factor_kernel(
    first_rows, first_cols, order, rrank, crank,
    weights, cols, cmask, wins, wmask, rows, rmask, pivots, trail,
    left, upper, solved, sums, win_left, cs, ws, rs,
):
    panels, bsize = weights.shape[0], weights.shape[1]
    narrow, rloc = cols.shape[0], cols.shape[1]
    f32, bf = jnp.float32, jnp.bfloat16
    step = pl.program_id(0)
    width = rows.shape[2]
    per = width // bsize

    def flag(condition):
        return jnp.where(condition, 1.0, 0.0).astype(f32)

    def rank(k):
        value = jnp.int32(0)
        for t in range(panels):
            value = value + jnp.where(order[t] == k, t, 0)
        return value

    ranks = [rank(k) for k in range(panels)]

    def band(k):
        return pl.ds(k * bsize, bsize)

    @pl.when(step == 0)
    def _():
        for n in range(narrow):
            cs[n] = cols[n].reshape(rloc * bsize, bsize)
            ws[n] = wins[n].reshape(panels * bsize, bsize)
        pv = [pivots[k] for k in range(panels)]
        for s in range(panels):
            k = order[s]
            weight = weights[k]
            at = band(s)
            left[:, at] = mm(cs[k], weight).astype(bf)
            for r in range(first_rows):
                left[band(r), at] = (left[band(r), at].astype(f32) * flag(rrank[r] > s)).astype(bf)
            lw = mm(ws[k], weight)
            for n in range(panels):
                part = lw[n * bsize:(n + 1) * bsize] * flag(ranks[n] > s)
                win_left[s, band(n), :] = part.astype(bf)
            source = pv[panels - 1].astype(f32)
            for n in range(panels - 1):
                source = jnp.where(k == n, pv[n].astype(f32), source)
            z = mm_t(weight, source.astype(bf)).astype(bf)
            solved[at, :] = z
            if s + 1 < panels:
                for n in range(narrow):
                    u = mm_t(weight, ws[n, pl.ds(pl.multiple_of(k * bsize, bsize), bsize), :])
                    u = (u * flag(ranks[n] > s)).astype(bf)
                    change = mm(left[:, at], u).reshape(rloc, bsize, bsize) * cmask[n][:, None, :]
                    old = cs[n].astype(f32)
                    cs[n] = (old - change.reshape(rloc * bsize, bsize)).astype(bf)
                    change = mm(win_left[s], u).reshape(panels, bsize, bsize)
                    change = change * wmask[n][:, 0:1, :]
                    old = ws[n].astype(f32)
                    ws[n] = (old - change.reshape(panels * bsize, bsize)).astype(bf)
                for n in range(panels):
                    change = mm(win_left[s, band(n), :], z)
                    pv[n] = (pv[n].astype(f32) - change).astype(bf)
        total = jnp.zeros(sums.shape, f32)
        for r in range(rloc):
            x = trail[r]
            if r < first_rows:
                x = (x.astype(f32) * flag(rrank[r] == panels)).astype(bf)
            total = total + mm_t(left[band(r), :], x)
        sums[...] = total

    for k in range(panels):
        rs[band(k), :] = rows[k]
    lane = lax.broadcasted_iota(jnp.int32, (1, width), 1) // bsize + step * per
    masks = []
    for k in range(panels):
        m = rmask[k]
        masks.append(jnp.concatenate([m[i:i + 1] for i in range(per)], axis=1))
    for s in range(panels):
        k = order[s]
        u = mm_t(weights[k], rs[pl.ds(pl.multiple_of(k * bsize, bsize), bsize), :])
        live = jnp.ones((1, width), f32)
        for c in range(first_cols):
            live = jnp.where(lane == c, flag(crank[c] > s), live)
        u = (u * live).astype(bf)
        upper[band(s), :] = u
        if s + 1 < panels:
            for n in range(panels):
                change = mm(win_left[s, band(n), :], u) * masks[n]
                rs[band(n), :] = (rs[band(n), :].astype(f32) - change).astype(bf)


def factor(order, rrank, crank, weights, gathered, trail):
    rows, _, rmask, pivots, cols, cmask, wins, wmask = gathered
    panels, bsize, total = rows.shape
    nwide, nnarrow = lax.axis_size("wide"), lax.axis_size("narrow")
    rloc, nrhs = trail.shape[0], trail.shape[2]
    bf, f32 = jnp.bfloat16, jnp.float32
    smem = pl.BlockSpec(memory_space=pltpu.SMEM)
    deep = panels * bsize

    def whole(shape):
        return pl.BlockSpec(shape, lambda i: (0,) * len(shape))

    return pl.pallas_call(
        functools.partial(factor_kernel, -(-panels // nwide), -(-panels // nnarrow)),
        grid=(total // CHUNK,),
        in_specs=[smem] * 3 + [
            whole(weights.shape), whole(cols.shape), whole(cmask.shape),
            whole(wins.shape), whole(wmask.shape),
            pl.BlockSpec((panels, bsize, CHUNK), lambda i: (0, 0, i)),
            pl.BlockSpec((panels, CHUNK // bsize, 128), lambda i: (0, i, 0)),
            whole(pivots.shape), whole(trail.shape),
        ],
        out_specs=(
            whole((rloc * bsize, deep)), pl.BlockSpec((deep, CHUNK), lambda i: (0, i)),
            whole((deep, nrhs)), whole((deep, nrhs)), whole((panels, deep, bsize)),
        ),
        out_shape=(
            jax.ShapeDtypeStruct((rloc * bsize, deep), bf),
            jax.ShapeDtypeStruct((deep, total), bf),
            jax.ShapeDtypeStruct((deep, nrhs), bf),
            jax.ShapeDtypeStruct((deep, nrhs), f32),
            jax.ShapeDtypeStruct((panels, deep, bsize), bf),
        ),
        scratch_shapes=[
            pltpu.VMEM((nnarrow, rloc * bsize, bsize), bf),
            pltpu.VMEM((nnarrow, deep, bsize), bf),
            pltpu.VMEM((deep, CHUNK), bf),
        ],
        compiler_params=pltpu.CompilerParams(vmem_limit_bytes=48 * 2**20),
        name="factor_panels",
    )(order, rrank, crank, weights, cols, cmask, wins, wmask, rows, rmask, pivots, trail)


def update_kernel(
    order, weights, left, upper, solved, sums, win_left, front, mask, right,
    front_out, right_out, window, acc,
):
    panels, bsize = weights.shape[0], weights.shape[1]
    group, cloc = front.shape[0], front.shape[2]
    f32, bf = jnp.float32, jnp.bfloat16
    tall = group * bsize

    @pl.when(pl.program_id(0) == 0)
    def _():
        window[...] = jnp.zeros_like(window)
        for s in reversed(range(panels)):
            k = order[s]
            at = pl.ds(s * bsize, bsize)
            stack = window[...].reshape(panels * bsize, window.shape[2])
            total = sums[at, :] + mm_t(win_left[s], stack)
            corrected = (solved[at, :].astype(f32) - total).astype(bf)
            window[k] = mm(weights[k], corrected).astype(bf)

    factors = left[...]
    for pair in range(cloc // 2):
        product = mm(factors, upper[:, pair * 2 * bsize:(pair + 1) * 2 * bsize])
        acc[pl.ds(2 * pair, tall, stride=cloc), :] = product[:, :bsize]
        acc[pl.ds(2 * pair + 1, tall, stride=cloc), :] = product[:, bsize:]
    change = mm(factors, solved[...]).reshape(right.shape)
    right_out[...] = (right[...].astype(f32) - change).astype(bf)
    some = 8
    for g in range(group):
        keep = mask[g][None]

        @pl.loop(0, bsize // some)
        def _(i):
            start = pl.multiple_of(i * some, some)
            at = pl.ds(pl.multiple_of((g * bsize + start) * cloc, some * cloc), some * cloc)
            change = acc[at, :].reshape(some, cloc, bsize) * keep
            old = front[g, pl.ds(start, some)].astype(f32)
            front_out[g, pl.ds(start, some)] = (old - change).astype(bf)


def update(order, weights, factors, sums, front, mask, right):
    left, upper, solved, _, win_left = factors
    rloc, bsize, cloc, _ = front.shape
    panels, nrhs = weights.shape[0], right.shape[2]
    group = GROUP if rloc % GROUP == 0 else 1
    deep = left.shape[1]

    def whole(shape):
        return pl.BlockSpec(shape, lambda i: (0,) * len(shape))

    front_spec = pl.BlockSpec((group, bsize, cloc, bsize), lambda i: (i, 0, 0, 0))
    right_spec = pl.BlockSpec((group, bsize, nrhs), lambda i: (i, 0, 0))
    return pl.pallas_call(
        update_kernel,
        grid=(rloc // group,),
        in_specs=[
            pl.BlockSpec(memory_space=pltpu.SMEM), whole(weights.shape),
            pl.BlockSpec((group * bsize, deep), lambda i: (i, 0)),
            whole(upper.shape), whole(solved.shape), whole(sums.shape), whole(win_left.shape),
            front_spec, pl.BlockSpec((group, cloc, bsize), lambda i: (i, 0, 0)), right_spec,
        ],
        out_specs=(front_spec, right_spec, whole((panels, bsize, nrhs))),
        out_shape=(
            jax.ShapeDtypeStruct(front.shape, jnp.bfloat16),
            jax.ShapeDtypeStruct(right.shape, jnp.bfloat16),
            jax.ShapeDtypeStruct((panels, bsize, nrhs), jnp.bfloat16),
        ),
        scratch_shapes=[pltpu.VMEM((group * bsize * cloc, bsize), jnp.float32)],
        compiler_params=pltpu.CompilerParams(vmem_limit_bytes=56 * 2**20),
        name="update_front",
    )(order, weights, left, upper, solved, sums, win_left, front, mask, right)


def body(front, pivot_inverse, rhs, trail_sol, block_mask, panel_order):
    rloc, bsize, cloc = front.shape[0], front.shape[2], front.shape[3]
    nrhs = rhs.shape[3]
    panels = panel_order.shape[0]
    nwide, nnarrow = lax.axis_size("wide"), lax.axis_size("narrow")
    blocks = front.reshape(rloc, bsize, cloc, bsize)
    right = rhs.reshape(rloc, bsize, nrhs)
    trail = trail_sol.reshape(rloc, bsize, nrhs)
    mask = block_mask.reshape(rloc, cloc).astype(jnp.float32)
    mask = jnp.broadcast_to(mask[:, :, None], (rloc, cloc, bsize))
    ids = jnp.arange(panels, dtype=jnp.int32)
    rows_global = jnp.arange(rloc, dtype=jnp.int32) * nwide + lax.axis_index("wide")
    cols_global = jnp.arange(cloc, dtype=jnp.int32) * nnarrow + lax.axis_index("narrow")

    def rank_of(index):
        return jnp.min(
            jnp.where(index[:, None] == panel_order[None, :], ids[None, :], panels), axis=1
        )

    gathered = gather(
        blocks[0].reshape(bsize, cloc * bsize), right, blocks[:, :, 0, :],
        mask[:, 0, :], mask[0], panels,
    )
    factors = factor(
        panel_order, rank_of(rows_global), rank_of(cols_global), pivot_inverse, gathered, trail
    )
    sums = reduce_sums(factors[3].reshape(panels, bsize, nrhs)).reshape(panels * bsize, nrhs)
    blocks, right, window = update(
        panel_order, pivot_inverse, factors, sums, blocks, mask, right
    )
    return (blocks.reshape(front.shape), right.reshape(rhs.shape), window)


def solution(mesh):
    in_specs = (
        P(None, "wide", None, None, "narrow", None),
        P(),
        P(None, "wide", None, None),
        P(None, "wide", None, None),
        P(None, "wide", None, "narrow"),
        P(),
    )
    out_specs = (P(None, "wide", None, None, "narrow", None), P(None, "wide", None, None), P())
    return jax.shard_map(body, mesh=mesh, in_specs=in_specs, out_specs=out_specs, check_vma=False)
```
